256 devices in a mesh: dp: 4 (over x_lo, core), ctx: 64 (over x_hi, z, y).
Axes of the slice: x: 4 (x_hi: 2, x_lo: 2; x = x_hi * 2 + x_lo), y: 4, z: 8, core: 2. Of those that a mesh axis runs over, the one named last changes fastest.
Arguments:
- queries: bfloat16 [65536, 512], P(('dp', 'ctx')), parts along dimension 0, may hold values from -9 to 9
- keys: bfloat16 [65536, 128], P(('dp', 'ctx')), parts along dimension 0, may hold values from -9 to 9
- values: bfloat16 [65536, 128], P(('dp', 'ctx')), parts along dimension 0, may hold values from -6 to 6
- lengths: int32 [32], P('dp'), parts along dimension 0, may hold values from 1 to 10240, 16384 in all
Outputs:
- attended: bfloat16 [65536, 512], P(('dp', 'ctx')), parts along dimension 0
- log_norm: float32 [4, 65536], P(None, ('dp', 'ctx')), parts along dimension 1
The draws below stay inside these ranges and needn't reach their ends.
There are 4 independent parts, one for each index of `dp`. The reference program is written for one: setup_inputs(seed, part) draws one part's arguments, and reference() takes and returns one part's arrays. A program takes and returns all parts, laid end to end along the dimension named above; each array names one. Nothing has to cross between parts.
Inputs may be any that keep to these rules, and one draw needn't show every extreme that they name: The 8 lengths sum to 16384, and the largest is exactly 10240.
All inputs are finite; a program needn't handle non-finite values.
Results may differ from the reference program's by a relative error of at most 0.0045.
Values may be sent and summed in bfloat16 or wider, within the bound.
No kernel may reach another device: no remote copies, remote signals or barrier semaphores. Data moves between devices by JAX's collectives and lax.ppermute only.
A program may use at most 64 MiB of HBM per device.

```python
import math
import jax
import jax.numpy as jnp
import numpy as np
from jax import lax

H = 4
DH = 128
NDOC = 8
SEQ = 16384
MOST = 10240


def draw_queries(key, part):
    key = jax.random.fold_in(key, 11)
    base = jnp.clip(1.4 * jax.random.normal(key, (SEQ, H * DH), jnp.float32), -9.0, 9.0)
    return base.astype(jnp.bfloat16)


def draw_keys(key, part):
    key = jax.random.fold_in(key, 23)
    base = jnp.clip(1.4 * jax.random.normal(key, (SEQ, DH), jnp.float32), -9.0, 9.0)
    return base.astype(jnp.bfloat16)


def steps_of(rng, shape, cuts, least, top_value):
    def one(axis_at, parts):
        steps = jax.random.uniform(jax.random.fold_in(jax.random.fold_in(rng, 6), axis_at), (parts,), jnp.float32, least / len(cuts), top_value / len(cuts))
        return jnp.repeat(jnp.exp(steps), shape[axis_at] // parts).reshape((-1,) + (1,) * (len(shape) - axis_at - 1))

    factor_of = one(*cuts[0])
    for cut in cuts[1:]:
        factor_of = factor_of * one(*cut)
    return factor_of


def profile(number_of, total, limit, skew):
    portions = [(1 << 20) // math.isqrt(rank ** skew) + 1 for rank in range(2, number_of + 1)]
    spare, counts = total - limit - (number_of - 1), [1] * (number_of - 1)
    while spare > 0:
        movable = [i for i in range(number_of - 1) if counts[i] < limit]
        pool, budget = sum([portions[i] for i in movable]), spare
        for i in movable:
            extra = min(limit - counts[i], max(1, budget * portions[i] // pool), spare)
            counts[i] = counts[i] + extra
            spare = spare - extra
    return np.array([limit] + counts)


def uneven(own_key, amount, total, limit, skew):
    if amount == 2:
        one = jax.random.randint(own_key, (), max(1, total - limit), min(limit, total - 1) + 1)
        return jnp.stack([one, total - one])
    sizes = jnp.asarray(profile(amount, total, limit, skew), jnp.int32)
    twos = (amount - 1) // 2
    giver, receiver = sizes[1:1 + 2 * twos:2], sizes[2:2 + 2 * twos:2]
    slack = jnp.minimum(giver - 1, limit - receiver)
    passed = jax.random.randint(jax.random.fold_in(own_key, 1), (twos,), 0, 1 << 20) % (slack + 1)
    sizes = sizes.at[1:1 + 2 * twos:2].set(giver - passed).at[2:2 + 2 * twos:2].set(receiver + passed)
    return sizes[jax.random.permutation(jax.random.fold_in(own_key, 2), amount)]


def normal_values(key, extent, width, bound, pieces=(), held_as=jnp.bfloat16):
    level = steps_of(key, extent, pieces, -0.22, 0.18) if pieces else 1.0
    values = jax.random.normal(key, extent, jnp.float32) * width * level
    return jnp.minimum(jnp.maximum(values, -bound), bound).astype(held_as)


def setup_inputs(seed: int = 0, part: int = 0) -> dict:
    streams_of = jax.random.split(jax.random.key(seed), 5)
    part_splits = jax.random.split(jax.random.fold_in(streams_of[4], part), 5)
    queries = draw_queries(jax.random.fold_in(jax.random.fold_in(streams_of[4], part), 71), part)
    keys = draw_keys(jax.random.fold_in(jax.random.fold_in(streams_of[4], part), 71), part)
    values = normal_values(part_splits[2], (SEQ, DH), 1.0, 6.0, ((0, 64),))
    lengths = uneven(part_splits[3], NDOC, SEQ, MOST, 1).astype(jnp.int32)
    return {"queries": queries, "keys": keys, "values": values, "lengths": lengths}


NEG_FILL = -1e+30

def document_ids(lengths, positions):
    doc_ends = jnp.cumsum(lengths).astype(jnp.int32)
    return lax.optimization_barrier(jnp.sum((positions[:, None] >= doc_ends[None, :]).astype(jnp.int32), axis=1)).astype(jnp.int32)

def reference(queries, keys, values, lengths):
    positions = jnp.arange(SEQ, dtype=jnp.int32)
    doc_id = document_ids(lengths, positions)
    block_rows = math.gcd(SEQ, 512)
    score_scale = jnp.float32(1.0 / math.sqrt(DH))
    keys_wide = keys.astype(jnp.float32)
    values_wide = values.astype(jnp.float32)

    def one_block(number):
        first = number * block_rows
        query_block = lax.dynamic_slice_in_dim(queries, first, block_rows, 0)
        query_pos = lax.dynamic_slice_in_dim(positions, first, block_rows, 0)
        query_doc = lax.dynamic_slice_in_dim(doc_id, first, block_rows, 0)
        query_heads = query_block.reshape(block_rows, H, DH).astype(jnp.float32)
        scores = jnp.einsum('qhd,kd->hqk', query_heads, keys_wide) * score_scale
        allowed = (query_doc[:, None] == doc_id[None, :]) & (positions[None, :] <= query_pos[:, None])
        scores = jnp.where(allowed[None], scores, NEG_FILL)
        row_max = lax.optimization_barrier(jnp.max(scores, axis=-1))
        weights = jnp.where(allowed[None], jnp.exp(scores - row_max[..., None]), jnp.float32(0.0))
        row_sum = lax.optimization_barrier(jnp.sum(weights, axis=-1))
        weights_low = weights.astype(jnp.bfloat16)
        numerator = jnp.einsum('hqk,kd->qhd', weights_low.astype(jnp.float32), values_wide)
        attended = (numerator / jnp.transpose(row_sum)[:, :, None]).reshape(block_rows, H * DH).astype(jnp.bfloat16)
        log_norm = row_max + jnp.log(row_sum)
        return (attended, log_norm)
    outputs, norms = lax.map(one_block, jnp.arange(SEQ // block_rows, dtype=jnp.int32))
    attended = outputs.reshape(SEQ, H * DH)
    log_norm = jnp.transpose(norms, (1, 0, 2)).reshape(H, SEQ)
    return (attended, log_norm)
```

```python
import functools
import math

import jax
import jax.numpy as jnp
from jax import lax
from jax.experimental import pallas as pl
from jax.experimental.pallas import tpu as pltpu
from jax.sharding import PartitionSpec as P

X, Z, Y = 2, 8, 4
ROWS = 256
HEADS = 4
DIM = 128
EXT = DIM + 16
ROW_SPAN = Y * ROWS
BAND = 10
FAR = 1 << 24
NEG = -1e30
FLOOR = -1e29
CHUNK = 4
SCALE = 1.0 / math.sqrt(DIM)
EXP2_SCALE = SCALE * math.log2(math.e)


def index_of(x, z, y):
    return x * (Z * Y) + (z % Z) * Y + (y % Y)


def y_pairs(step):
    return [
        (index_of(x, z, y), index_of(x, z, y + step))
        for x in range(X)
        for z in range(Z)
        for y in range(Y)
    ]


def needed(x, z, own, z_from):
    row, other = x * Z + z, own * Z + z_from % Z
    return other < row and row - other <= BAND


def z_moves(x_of, own):
    late = {1: [], -1: []}
    early = {1: [], -1: [], 4: []}
    wanted = set()
    for x in x_of:
        mine = x if own is None else own
        for z in range(Z):
            for step in (1, -1):
                via = (z - step) % Z
                sent = [via - step, via + 4]
                if any(needed(x, z, mine, b) for b in sent):
                    late[step].append((x, via, z))
                    if needed(x, z, mine, sent[0]):
                        wanted.add((x, via, step))
                    if needed(x, z, mine, sent[1]):
                        wanted.add((x, via, 4))
            for step in (1, -1, 4):
                if needed(x, z, mine, z - step):
                    wanted.add((x, z, step))
    for x, z, step in sorted(wanted):
        early[step].append((x, (z - step) % Z, z))
    expand = lambda moves: [
        (index_of(x, a, y), index_of(x, b, y)) for x, a, b in moves for y in range(Y)
    ]
    return {s: expand(m) for s, m in early.items()}, {s: expand(m) for s, m in late.items()}


def doc_start(lengths_ref, position):
    start = position * 0
    end = jnp.int32(0)
    for k in range(8):
        size = lengths_ref[k]
        end = end + size
        start = start + jnp.where(position >= end, size, 0)
    return start


def attend(steps, places, carried, finish, *refs):
    nq = len(steps)
    flat = [p for group in places for p in group]
    nb = len(flat)
    refs = list(refs)
    lengths_ref = refs.pop(0)
    q_refs = [refs.pop(0) for _ in range(1 if carried else nq)]
    kv_refs = [refs.pop(0) for _ in places]
    if carried:
        acc_in, top_in = refs.pop(0), refs.pop(0)
    if finish:
        message_refs = [refs.pop(0) for _ in range(nq)]
        acc, top = refs.pop(), refs.pop()
    else:
        acc, top = refs.pop(0), refs.pop(0)
    qt = q_refs[0] if carried else refs.pop(0)
    ks, vt, key_at = refs

    me = lax.axis_index("ctx")
    x, z, y = me // (Z * Y), (me // Y) % Z, me % Y
    row_low = (x * Z + z) * ROW_SPAN
    row_high = row_low + (ROW_SPAN - 1)
    low = doc_start(lengths_ref, row_low)
    high = doc_start(lengths_ref, row_high)

    if not carried:
        for n in range(nq):
            for h in range(HEADS):
                qt[n * HEADS + h] = q_refs[n][:, h * DIM : (h + 1) * DIM].T

    n_whole, n_part = jnp.int32(0), jnp.int32(0)
    n = 0
    for ref, group in zip(kv_refs, places):
        for part in range(len(group)):
            kind, dz = flat[n]
            z_from = (z + dz + Z) % Z
            if kind == 0:
                k0 = (x * Z + z_from) * ROW_SPAN + y * ROWS
            else:
                k0 = jnp.where(x == 1, z_from * ROW_SPAN + y * ROWS, FAR)
            some = (k0 <= row_high) & (k0 + (ROWS - 1) >= low)
            whole = (k0 + (ROWS - 1) <= row_low) & (k0 >= high)
            slot = jnp.where(whole, n_whole, nb - 1 - n_part)

            @pl.when(some)
            def _(ref=ref, part=part, k0=k0, slot=slot):
                keys = slice(2 * part * ROWS, (2 * part + 1) * ROWS)
                values = slice((2 * part + 1) * ROWS, (2 * part + 2) * ROWS)
                at = pl.ds(pl.multiple_of(slot * ROWS, ROWS), ROWS)
                key_at[slot] = k0
                ks[at, :] = ref[keys, :]
                vt[:DIM, at] = ref[values, :].T

            n_whole = n_whole + jnp.where(some & whole, 1, 0)
            n_part = n_part + jnp.where(some & jnp.logical_not(whole), 1, 0)
            n += 1
    vt[DIM:, :] = jnp.ones((EXT - DIM, nb * ROWS), jnp.bfloat16)

    if carried:
        acc[...] = acc_in[...]
        top[...] = top_in[...]
    else:
        acc[...] = jnp.zeros(acc.shape, jnp.float32)
        top[...] = jnp.full(top.shape, FLOOR, jnp.float32)

    def one_query_block(qb, _):
        t0 = qb * HEADS
        step = steps[0]
        for n in range(1, nq):
            step = jnp.where(qb == n, steps[n], step)
        q0 = row_low + ((y + step + Y) % Y) * ROWS

        def update(slot, count, masked):
            at = pl.ds(pl.multiple_of(slot * ROWS, ROWS), count * ROWS)
            k, v = ks[at, :], vt[:, at]
            if masked:
                query_pos = q0 + lax.broadcasted_iota(jnp.int32, (1, ROWS), 1)
                key_pos = key_at[slot] + lax.broadcasted_iota(jnp.int32, (ROWS, ROWS), 0)
                allowed = (key_pos >= doc_start(lengths_ref, query_pos)) & (key_pos <= query_pos)
            olds = [top[t0 + h] for h in range(HEADS)]
            scores = [
                jnp.dot(k, qt[t0 + h], preferred_element_type=jnp.float32) for h in range(HEADS)
            ]
            if masked:
                scores = [jnp.where(allowed, s, NEG) for s in scores]
            news = [
                jnp.maximum(o, jnp.max(s, axis=0, keepdims=True)) for o, s in zip(olds, scores)
            ]
            weights = [
                jnp.exp2((s - n) * EXP2_SCALE).astype(jnp.bfloat16) for s, n in zip(scores, news)
            ]
            sums = [jnp.dot(v, w, preferred_element_type=jnp.float32) for w in weights]
            sums = [
                acc[t0 + h] * jnp.exp2((olds[h] - news[h]) * EXP2_SCALE) + sums[h]
                for h in range(HEADS)
            ]
            for h in range(HEADS):
                top[t0 + h] = news[h]
                acc[t0 + h] = sums[h]

        done = 0
        if nb >= CHUNK:
            def one_chunk(c, _):
                update(c * CHUNK, CHUNK, False)
                return 0

            lax.fori_loop(0, n_whole // CHUNK, one_chunk, 0)
            done = (n_whole // CHUNK) * CHUNK
        for count in (2, 1):
            if nb >= count:
                here = done

                @pl.when((n_whole - here) >= count)
                def _(count=count, here=here):
                    update(here, count, False)

                done = here + jnp.where((n_whole - here) >= count, count, 0)

        first = doc_start(lengths_ref, q0)

        def one_part(n, _):
            slot = nb - 1 - n
            k0 = key_at[slot]

            @pl.when((k0 <= q0 + (ROWS - 1)) & (k0 + (ROWS - 1) >= first))
            def _():
                update(slot, 1, True)

            return 0

        lax.fori_loop(0, n_part, one_part, 0)
        return 0

    lax.fori_loop(0, nq, one_query_block, 0)

    if finish:
        for n in range(nq):
            for h in range(HEADS):
                t = n * HEADS + h
                at = slice(h * ROWS, (h + 1) * ROWS)
                total = acc[t, DIM : DIM + 1]
                some = total > 0
                total = jnp.where(some, total, 1.0)
                log_norm = jnp.where(some, top[t] * SCALE + jnp.log(total), NEG)
                message_refs[n][:DIM, at] = (acc[t, :DIM] * (1.0 / total)).astype(jnp.bfloat16)
                first = log_norm.astype(jnp.bfloat16)
                rest = log_norm - first.astype(jnp.float32)
                second = rest.astype(jnp.bfloat16)
                third = (rest - second.astype(jnp.float32)).astype(jnp.bfloat16)
                row = lax.broadcasted_iota(jnp.int32, (EXT - DIM, ROWS), 0)
                pieces = jnp.where(
                    row == 0,
                    first.astype(jnp.float32),
                    jnp.where(row == 1, second.astype(jnp.float32), third.astype(jnp.float32)),
                )
                message_refs[n][DIM:, at] = pieces.astype(jnp.bfloat16)


def run_attend(lengths, queries, steps, arrays, places, carry, finish):
    nq, nb = len(steps), sum(len(g) for g in places)
    tiles = nq * HEADS
    vmem = pl.BlockSpec(memory_space=pltpu.VMEM)
    acc = jax.ShapeDtypeStruct((tiles, EXT, ROWS), jnp.float32)
    top = jax.ShapeDtypeStruct((tiles, 1, ROWS), jnp.float32)
    turned = jax.ShapeDtypeStruct((tiles, DIM, ROWS), jnp.bfloat16)
    scratch = [
        pltpu.VMEM((nb * ROWS, DIM), jnp.bfloat16),
        pltpu.VMEM((EXT, nb * ROWS), jnp.bfloat16),
        pltpu.SMEM((nb,), jnp.int32),
    ]
    if finish:
        out_shape = [jax.ShapeDtypeStruct((EXT, HEADS * ROWS), jnp.bfloat16)] * nq
        scratch += [pltpu.VMEM(top.shape, top.dtype), pltpu.VMEM(acc.shape, acc.dtype)]
    else:
        out_shape = [acc, top, turned]
    operands = [lengths, *queries, *arrays, *(carry or ())]
    units = nq * nb * HEADS * ROWS * ROWS
    return pl.pallas_call(
        functools.partial(attend, steps, places, carry is not None, finish),
        out_shape=out_shape,
        in_specs=[pl.BlockSpec(memory_space=pltpu.SMEM)] + [vmem] * (len(operands) - 1),
        out_specs=[vmem] * len(out_shape),
        scratch_shapes=scratch,
        compiler_params=pltpu.CompilerParams(vmem_limit_bytes=48 << 20),
        cost_estimate=pl.CostEstimate(
            flops=units * DIM * 2, bytes_accessed=1 << 20, transcendentals=units // 2
        ),
    )(*operands)


def merge(acc, top, *refs):
    *received, out, norm = refs
    for h in range(HEADS):
        at = slice(h * ROWS, (h + 1) * ROWS)
        own_total = acc[h, DIM : DIM + 1]
        logs = [top[h] * SCALE + jnp.log(own_total)]
        for r in received:
            pieces = r[DIM:, at].astype(jnp.float32)
            logs.append(pieces[0:1] + pieces[1:2] + pieces[2:3])
        most = functools.reduce(jnp.maximum, logs)
        parts = [jnp.exp(v - most) for v in logs]
        total = sum(parts)
        mixed = acc[h, :DIM] * (parts[0] / (own_total * total))
        for r, part in zip(received, parts[1:]):
            mixed = mixed + r[:DIM, at].astype(jnp.float32) * (part / total)
        out[:, h * DIM : (h + 1) * DIM] = mixed.T.astype(jnp.bfloat16)
        norm[h : h + 1, :] = most + jnp.log(total)


def run_merge(acc, top, received):
    vmem = pl.BlockSpec(memory_space=pltpu.VMEM)
    return pl.pallas_call(
        merge,
        out_shape=[
            jax.ShapeDtypeStruct((ROWS, HEADS * DIM), jnp.bfloat16),
            jax.ShapeDtypeStruct((HEADS, ROWS), jnp.float32),
        ],
        in_specs=[vmem] * (2 + len(received)),
        out_specs=[vmem] * 2,
        compiler_params=pltpu.CompilerParams(vmem_limit_bytes=24 << 20),
    )(acc, top, *received)


def gather_z(block, x_of, own):
    early, late = z_moves(x_of, own)
    from_below = lax.ppermute(block, "ctx", early[1])
    from_above = lax.ppermute(block, "ctx", early[-1])
    from_far = lax.ppermute(block, "ctx", early[4])
    up = lax.ppermute(jnp.concatenate([from_below, from_far], 0), "ctx", late[1])
    down = lax.ppermute(jnp.concatenate([from_above, from_far], 0), "ctx", late[-1])
    first = [(from_below, [-1]), (from_above, [1]), (from_far, [4])]
    second = [(up, [-2, 3]), (down, [2, -3])]
    return first, second


def shards(queries, keys, values, lengths):
    block = jnp.concatenate([keys, values], axis=0)
    across = [(index_of(0, z, y), index_of(1, z, y)) for z in range(Z) for y in range(Y)]
    steps = (-1, 1, 2)
    partner = lax.ppermute(block, "ctx", across)
    own_first, own_second = gather_z(block, (0, 1), None)
    other_queries = [lax.ppermute(queries, "ctx", y_pairs(-s)) for s in steps]
    low_first, low_second = gather_z(partner, (1,), 0)

    tag = lambda kind, groups: [(a, [(kind, dz) for dz in offs]) for a, offs in groups]
    most = tag(0, [(block, [0])] + own_first + own_second) + tag(1, [(partner, [0])] + low_first)
    rest = tag(1, low_second)
    unzip = lambda pairs: ([a for a, _ in pairs], [p for _, p in pairs])
    acc, top, turned = run_attend(lengths, other_queries, steps, *unzip(most), None, False)
    messages = run_attend(lengths, [turned], steps, *unzip(rest), (acc, top), True)
    received = [lax.ppermute(m, "ctx", y_pairs(s)) for m, s in zip(messages, steps)]
    acc, top, _ = run_attend(lengths, [queries], (0,), *unzip(most + rest), None, False)
    return tuple(run_merge(acc, top, received))


def solution(mesh):
    in_specs = (P(("dp", "ctx"), None), P(("dp", "ctx"), None), P(("dp", "ctx"), None), P("dp"))
    out_specs = (P(("dp", "ctx"), None), P(None, ("dp", "ctx")))
    return jax.shard_map(shards, mesh=mesh, in_specs=in_specs, out_specs=out_specs, check_vma=False)
```

```python
import functools
import math

import jax
import jax.numpy as jnp
from jax import lax
from jax.experimental import pallas as pl
from jax.experimental.pallas import tpu as pltpu
from jax.sharding import PartitionSpec as P

X, Z, Y = 2, 8, 4
ROWS = 256
HEADS = 4
DIM = 128
EXT = DIM + 16
ROW_SPAN = Y * ROWS
BAND = 10
FAR_ROW = 1 << 14
NEG = -1e30
FLOOR = -1e29
CHUNK = 4
EXP2_SCALE = math.log2(math.e) / math.sqrt(DIM)
LOG_2 = math.log(2.0)


def index_of(x, z, y):
    return x * (Z * Y) + (z % Z) * Y + (y % Y)


def y_pairs(step):
    return [
        (index_of(x, z, y), index_of(x, z, y + step))
        for x in range(X)
        for z in range(Z)
        for y in range(Y)
    ]


COLUMNS = range(X)
NEXT = [((c, z), (c, z + 1)) for c in COLUMNS for z in range(Z - 1)]
LOW_NEXT = [((0, z), (1, (z + 1) % Z)) for z in range(Z)]
BACK = [((0, z), (1, z - 1)) for z in range(1, Z)] + [((c, 0), (c, Z - 1)) for c in COLUMNS]
HALF = [((c, z), (c, z + 4)) for c in COLUMNS for z in range(4)]
HALF += [((0, z), (1, z - 4)) for z in range(4, Z)]
EXTRA_ONE = [((c, 1), (c, Z - 1)) for c in COLUMNS]
EXTRA_FOUR = [((c, 4), (c, Z - 1)) for c in COLUMNS] + [((0, 3), (1, 0))]
UP = [((0, z), (0, z + 1)) for z in range(1, Z - 1)] + [((1, z), (1, (z + 1) % Z)) for z in range(Z)]
DOWN = [((0, z), (0, z - 1)) for z in range(4, Z)] + [((1, z), (1, (z - 1) % Z)) for z in range(Z)]


def move(block, pairs):
    along = [(index_of(*a, y), index_of(*b, y)) for a, b in pairs for y in range(Y)]
    return lax.ppermute(block, "ctx", along)


def own_row(step):
    return lambda x, z: x * Z + (z + step + Z) % Z


def low_row(step):
    return lambda x, z: jnp.where(x == 1, (z + step + Z) % Z, FAR_ROW)


def half_row(step):
    def row(x, z):
        at = x * Z + (z + step + Z) % Z - 4
        return jnp.where(at >= 0, at, FAR_ROW)

    return row


def back_row(step):
    def row(x, z):
        via = (z + step + Z) % Z
        return jnp.where(x == 1, via + 1, jnp.where(via == Z - 1, 0, FAR_ROW))

    return row


def extra_one_row(x, z):
    return jnp.where(z == Z - 1, x * Z + 1, FAR_ROW)


def extra_four_row(x, z):
    return jnp.where(z == Z - 1, x * Z + 4, jnp.where((z == 0) & (x == 1), 3, FAR_ROW))


def gather(block):
    below, low_next = move(block, NEXT), move(block, LOW_NEXT)
    back, half = move(block, BACK), move(block, HALF)
    extra_one, extra_four = move(block, EXTRA_ONE), move(block, EXTRA_FOUR)
    up = move(jnp.concatenate([below, low_next, half], 0), UP)
    down = move(jnp.concatenate([back, half, low_next], 0), DOWN)
    first = [
        (block, [own_row(0)]),
        (below, [own_row(-1)]),
        (low_next, [low_row(-1)]),
        (back, [back_row(0)]),
        (half, [half_row(0)]),
        (extra_one, [extra_one_row]),
        (extra_four, [extra_four_row]),
    ]
    second = [(up, [own_row(-2), low_row(-2), half_row(-1)]), (down, [back_row(1), half_row(1), low_row(0)])]
    return first, second


def doc_start(lengths_ref, position):
    start = position * 0
    end = jnp.int32(0)
    for k in range(8):
        size = lengths_ref[k]
        end = end + size
        start = start + jnp.where(position >= end, size, 0)
    return start


def attend(steps, places, carried, finish, tile, *refs):
    nq = len(steps)
    flat = [p for group in places for p in group]
    nb = len(flat)
    refs = list(refs)
    lengths_ref = refs.pop(0)
    q_refs = [refs.pop(0) for _ in range(nq)]
    kv_refs = [refs.pop(0) for _ in places]
    if carried:
        acc_in, top_in = refs.pop(0), refs.pop(0)
    if finish:
        message_refs = [refs.pop(0) for _ in range(nq)]
        acc, top = refs.pop(), refs.pop()
    else:
        acc, top = refs.pop(0), refs.pop(0)
    qt, ks, vt, key_at, seen = refs

    me = lax.axis_index("ctx")
    x, z, y = me // (Z * Y), (me // Y) % Z, me % Y
    row = x * Z + z
    row_low = row * ROW_SPAN
    row_high = row_low + (ROW_SPAN - 1)
    low = doc_start(lengths_ref, row_low)

    for n in range(nq):
        for h in range(HEADS):
            scaled = q_refs[n][:, h * DIM : (h + 1) * DIM].T.astype(jnp.float32) * EXP2_SCALE
            high = scaled.astype(jnp.bfloat16)
            qt[n * HEADS + h, :DIM] = high
            qt[n * HEADS + h, DIM:] = (scaled - high.astype(jnp.float32)).astype(jnp.bfloat16)

    for d in range(BAND + 2):
        seen[d] = 0
    for n in range(nb):
        key_at[n] = -FAR_ROW * ROW_SPAN
    starts, places_of = [], []
    for row_of in flat:
        row_from = row_of(x, z)
        k0 = row_from * ROW_SPAN + y * ROWS
        counts = (k0 <= row_high) & (k0 + (ROWS - 1) >= low)
        place = jnp.where(counts, row - row_from, BAND + 1)
        seen[place] = 1
        starts.append(k0)
        places_of.append(place)
    n_slots = jnp.int32(0)
    for d in range(BAND + 1):
        here = seen[d]
        seen[d] = n_slots
        n_slots = n_slots + here
    n = 0
    for ref, group in zip(kv_refs, places):
        for part in range(len(group)):

            @pl.when(places_of[n] <= BAND)
            def _(ref=ref, part=part, k0=starts[n], place=places_of[n]):
                slot = seen[place]
                base = 2 * part * ROWS
                key_at[slot] = k0
                at = pl.multiple_of(slot * ROWS, ROWS)
                for half in range(2):
                    ks[pl.ds(at, ROWS), half * DIM : (half + 1) * DIM] = ref[base : base + ROWS, :]
                for half in range(2):
                    rows = base + ROWS + half * DIM
                    vt[:DIM, pl.ds(pl.multiple_of(at + half * DIM, DIM), DIM)] = ref[rows : rows + DIM, :]

            n += 1
    vt[DIM:, :] = jnp.ones((EXT - DIM, nb * ROWS), jnp.bfloat16)

    if carried:
        acc[...] = acc_in[tile : tile + nq * HEADS]
        top[...] = top_in[tile : tile + nq * HEADS]
    else:
        acc[...] = jnp.zeros(acc.shape, jnp.float32)
        top[...] = jnp.full(top.shape, FLOOR, jnp.float32)

    def one_query_block(qb, _):
        t0 = qb * HEADS
        step = steps[0]
        for n in range(1, nq):
            step = jnp.where(qb == n, steps[n], step)
        q0 = row_low + ((y + step + Y) % Y) * ROWS
        first = doc_start(lengths_ref, q0)
        last = doc_start(lengths_ref, q0 + (ROWS - 1))

        def update(slot, count, masked):
            at = pl.ds(pl.multiple_of(slot * ROWS, ROWS), count * ROWS)
            k, v = ks[at, :], vt[:, at]
            if masked:
                query_pos = q0 + lax.broadcasted_iota(jnp.int32, (1, ROWS), 1)
                query_start = doc_start(lengths_ref, query_pos)
                key_pos = [
                    key_at[slot + i] + lax.broadcasted_iota(jnp.int32, (ROWS, ROWS), 0)
                    for i in range(count)
                ]
                key_pos = jnp.concatenate(key_pos, 0)
                allowed = (key_pos >= query_start) & (key_pos <= query_pos)
            olds = [top[t0 + h] for h in range(HEADS)]
            scores = [
                jnp.dot(k, qt[t0 + h], preferred_element_type=jnp.float32) for h in range(HEADS)
            ]
            if masked:
                scores = [jnp.where(allowed, s, NEG) for s in scores]
            news = [
                jnp.maximum(o, jnp.max(s, axis=0, keepdims=True)) for o, s in zip(olds, scores)
            ]
            weights = [
                jnp.exp2(s - n).astype(jnp.bfloat16) for s, n in zip(scores, news)
            ]
            sums = [jnp.dot(v, w, preferred_element_type=jnp.float32) for w in weights]
            sums = [
                acc[t0 + h] * jnp.exp2(olds[h] - news[h]) + sums[h]
                for h in range(HEADS)
            ]
            for h in range(HEADS):
                top[t0 + h] = news[h]
                acc[t0 + h] = sums[h]

        begin, near, inside, reach = (jnp.int32(0) for _ in range(4))
        for n in range(nb):
            k0 = key_at[n]
            begin = begin + jnp.where(k0 > q0 + (ROWS - 1), 1, 0)
            near = near + jnp.where(k0 + (ROWS - 1) > q0, 1, 0)
            inside = inside + jnp.where(k0 >= last, 1, 0)
            reach = reach + jnp.where(k0 + (ROWS - 1) >= first, 1, 0)

        def chunk(at, size):
            whole = (at >= near) & (at + size <= inside)
            pl.when(whole)(functools.partial(update, at, size, False))
            pl.when(jnp.logical_not(whole))(functools.partial(update, at, size, True))

        times = jnp.maximum(reach - begin, 0) // CHUNK

        def one_chunk(c, _):
            chunk(begin + c * CHUNK, CHUNK)
            return 0

        lax.fori_loop(0, times, one_chunk, 0)
        at = begin + times * CHUNK
        size = CHUNK // 2
        while size:
            some = reach - at >= size
            pl.when(some)(functools.partial(chunk, at, size))
            at = at + jnp.where(some, size, 0)
            size //= 2
        return 0

    lax.fori_loop(0, nq, one_query_block, 0)

    if finish:
        for n in range(nq):
            for h in range(HEADS):
                t = n * HEADS + h
                at = slice(h * ROWS, (h + 1) * ROWS)
                total = acc[t, DIM : DIM + 1]
                some = total > 0
                total = jnp.where(some, total, 1.0)
                log_norm = jnp.where(some, top[t] * LOG_2 + jnp.log(total), NEG)
                message_refs[n][:DIM, at] = (acc[t, :DIM] * (1.0 / total)).astype(jnp.bfloat16)
                first = log_norm.astype(jnp.bfloat16)
                rest = log_norm - first.astype(jnp.float32)
                second = rest.astype(jnp.bfloat16)
                third = (rest - second.astype(jnp.float32)).astype(jnp.bfloat16)
                row = lax.broadcasted_iota(jnp.int32, (EXT - DIM, ROWS), 0)
                pieces = jnp.where(
                    row == 0,
                    first.astype(jnp.float32),
                    jnp.where(row == 1, second.astype(jnp.float32), third.astype(jnp.float32)),
                )
                message_refs[n][DIM:, at] = pieces.astype(jnp.bfloat16)


def run_attend(lengths, queries, steps, arrays, places, carry, finish, tile=0):
    nq, nb = len(steps), sum(len(g) for g in places)
    tiles = nq * HEADS
    vmem = pl.BlockSpec(memory_space=pltpu.VMEM)
    acc = jax.ShapeDtypeStruct((tiles, EXT, ROWS), jnp.float32)
    top = jax.ShapeDtypeStruct((tiles, 1, ROWS), jnp.float32)
    scratch = [
        pltpu.VMEM((tiles, 2 * DIM, ROWS), jnp.bfloat16),
        pltpu.VMEM((nb * ROWS, 2 * DIM), jnp.bfloat16),
        pltpu.VMEM((EXT, nb * ROWS), jnp.bfloat16),
        pltpu.SMEM((nb,), jnp.int32),
        pltpu.SMEM((BAND + 2,), jnp.int32),
    ]
    if finish:
        out_shape = [jax.ShapeDtypeStruct((EXT, HEADS * ROWS), jnp.bfloat16)] * nq
        scratch += [pltpu.VMEM(top.shape, top.dtype), pltpu.VMEM(acc.shape, acc.dtype)]
    else:
        out_shape = [acc, top]
    operands = [lengths, *queries, *arrays, *(carry or ())]
    units = nq * nb * HEADS * ROWS * ROWS
    return pl.pallas_call(
        functools.partial(attend, steps, places, carry is not None, finish, tile),
        out_shape=out_shape,
        in_specs=[pl.BlockSpec(memory_space=pltpu.SMEM)] + [vmem] * (len(operands) - 1),
        out_specs=[vmem] * len(out_shape),
        scratch_shapes=scratch,
        compiler_params=pltpu.CompilerParams(vmem_limit_bytes=28 << 20),
        cost_estimate=pl.CostEstimate(
            flops=units * DIM * 2, bytes_accessed=1 << 20, transcendentals=units // 2
        ),
    )(*operands)


def turn_values(k_ref, v_ref, out_ref):
    out_ref[:ROWS, :] = k_ref[...]
    for half in range(2):
        at = ROWS + half * DIM
        out_ref[at : at + DIM, :] = v_ref[half * DIM : (half + 1) * DIM, :].T


def run_turn(kernel, shape, *operands):
    vmem = pl.BlockSpec(memory_space=pltpu.VMEM)
    return pl.pallas_call(
        kernel,
        out_shape=jax.ShapeDtypeStruct(shape, jnp.bfloat16),
        in_specs=[vmem] * len(operands),
        out_specs=vmem,
    )(*operands)


def merge(acc, top, *refs):
    *received, out, norm = refs
    for h in range(HEADS):
        at = slice(h * ROWS, (h + 1) * ROWS)
        own_total = acc[h, DIM : DIM + 1]
        logs = [top[h] * LOG_2 + jnp.log(own_total)]
        for r in received:
            pieces = r[DIM:, at].astype(jnp.float32)
            logs.append(pieces[0:1] + pieces[1:2] + pieces[2:3])
        most = functools.reduce(jnp.maximum, logs)
        parts = [jnp.exp(v - most) for v in logs]
        total = sum(parts)
        mixed = acc[h, :DIM] * (parts[0] / (own_total * total))
        for r, part in zip(received, parts[1:]):
            mixed = mixed + r[:DIM, at].astype(jnp.float32) * (part / total)
        out[:, h * DIM : (h + 1) * DIM] = mixed.T.astype(jnp.bfloat16)
        norm[h : h + 1, :] = most + jnp.log(total)


def run_merge(acc, top, received):
    vmem = pl.BlockSpec(memory_space=pltpu.VMEM)
    return pl.pallas_call(
        merge,
        out_shape=[
            jax.ShapeDtypeStruct((ROWS, HEADS * DIM), jnp.bfloat16),
            jax.ShapeDtypeStruct((HEADS, ROWS), jnp.float32),
        ],
        in_specs=[vmem] * (2 + len(received)),
        out_specs=[vmem] * 2,
        compiler_params=pltpu.CompilerParams(vmem_limit_bytes=24 << 20),
    )(acc, top, *received)


def shards(queries, keys, values, lengths):
    block = run_turn(turn_values, (2 * ROWS, DIM), keys, values)
    most, rest = gather(block)
    unzip = lambda pairs: ([a for a, _ in pairs], [p for _, p in pairs])
    steps = (-1, 1, 2)
    others = [lax.ppermute(queries, "ctx", y_pairs(-s)) for s in steps]
    received = []
    for low, high in ((0, 2), (2, 3)):
        group, these = steps[low:high], others[low:high]
        carry = run_attend(lengths, these, group, *unzip(most), None, False)
        messages = run_attend(lengths, these, group, *unzip(rest), carry, True)
        received += [lax.ppermute(m, "ctx", y_pairs(s)) for m, s in zip(messages, group)]
    acc, top = run_attend(lengths, [queries], (0,), *unzip(most + rest), None, False)
    return tuple(run_merge(acc, top, received))


def solution(mesh):
    in_specs = (P(("dp", "ctx"), None), P(("dp", "ctx"), None), P(("dp", "ctx"), None), P("dp"))
    out_specs = (P(("dp", "ctx"), None), P(None, ("dp", "ctx")))
    return jax.shard_map(shards, mesh=mesh, in_specs=in_specs, out_specs=out_specs, check_vma=False)
```

```python
import functools
import math

import jax
import jax.numpy as jnp
from jax import lax
from jax.experimental import pallas as pl
from jax.experimental.pallas import tpu as pltpu
from jax.sharding import PartitionSpec as P

X, Z, Y = 2, 8, 4
ROWS = 256
HEADS = 4
DIM = 128
EXT = DIM + 16
ROW_SPAN = Y * ROWS
BAND = 10
FAR_ROW = 1 << 14
NEG = -1e30
FLOOR = -1e29
CHUNK = 4
EXP2_SCALE = math.log2(math.e) / math.sqrt(DIM)
LOG_2 = math.log(2.0)


def index_of(x, z, y):
    return x * (Z * Y) + (z % Z) * Y + (y % Y)


def y_pairs(step):
    return [
        (index_of(x, z, y), index_of(x, z, y + step))
        for x in range(X)
        for z in range(Z)
        for y in range(Y)
    ]


COLUMNS = range(X)
NEXT = [((c, z), (c, z + 1)) for c in COLUMNS for z in range(Z - 1)]
LOW_NEXT = [((0, z), (1, (z + 1) % Z)) for z in range(Z)]
BACK = [((0, z), (1, z - 1)) for z in range(1, Z)] + [((c, 0), (c, Z - 1)) for c in COLUMNS]
HALF = [((c, z), (c, z + 4)) for c in COLUMNS for z in range(4)]
HALF += [((0, z), (1, z - 4)) for z in range(4, Z)]
EXTRA_ONE = [((c, 1), (c, Z - 1)) for c in COLUMNS]
EXTRA_FOUR = [((c, 4), (c, Z - 1)) for c in COLUMNS] + [((0, 3), (1, 0))]
UP = [((0, z), (0, z + 1)) for z in range(1, Z - 1)] + [((1, z), (1, (z + 1) % Z)) for z in range(Z)]
DOWN = [((0, z), (0, z - 1)) for z in range(4, Z)] + [((1, z), (1, (z - 1) % Z)) for z in range(Z)]


def move(block, pairs):
    along = [(index_of(*a, y), index_of(*b, y)) for a, b in pairs for y in range(Y)]
    return lax.ppermute(block, "ctx", along)


def own_row(step):
    return lambda x, z: x * Z + (z + step + Z) % Z


def low_row(step):
    return lambda x, z: jnp.where(x == 1, (z + step + Z) % Z, FAR_ROW)


def half_row(step):
    def row(x, z):
        at = x * Z + (z + step + Z) % Z - 4
        return jnp.where(at >= 0, at, FAR_ROW)

    return row


def back_row(step):
    def row(x, z):
        via = (z + step + Z) % Z
        return jnp.where(x == 1, via + 1, jnp.where(via == Z - 1, 0, FAR_ROW))

    return row


def extra_one_row(x, z):
    return jnp.where(z == Z - 1, x * Z + 1, FAR_ROW)


def extra_four_row(x, z):
    return jnp.where(z == Z - 1, x * Z + 4, jnp.where((z == 0) & (x == 1), 3, FAR_ROW))


def gather(block):
    below, low_next = move(block, NEXT), move(block, LOW_NEXT)
    back, half = move(block, BACK), move(block, HALF)
    extra_one, extra_four = move(block, EXTRA_ONE), move(block, EXTRA_FOUR)
    up = move(jnp.concatenate([below, low_next, half], 0), UP)
    down = move(jnp.concatenate([back, half, low_next], 0), DOWN)
    first = [
        (block, [own_row(0)]),
        (below, [own_row(-1)]),
        (low_next, [low_row(-1)]),
        (back, [back_row(0)]),
        (half, [half_row(0)]),
        (extra_one, [extra_one_row]),
        (extra_four, [extra_four_row]),
    ]
    second = [(up, [own_row(-2), low_row(-2), half_row(-1)]), (down, [back_row(1), half_row(1), low_row(0)])]
    return first, second


def doc_start(lengths_ref, position):
    start = position * 0
    end = jnp.int32(0)
    for k in range(8):
        size = lengths_ref[k]
        end = end + size
        start = start + jnp.where(position >= end, size, 0)
    return start


def attend(steps, places, carried, finish, tile, *refs):
    nq = len(steps)
    flat = [p for group in places for p in group]
    nb = len(flat)
    refs = list(refs)
    lengths_ref = refs.pop(0)
    q_refs = [refs.pop(0) for _ in range(nq)]
    kv_refs = [refs.pop(0) for _ in places]
    if carried:
        acc_in, top_in = refs.pop(0), refs.pop(0)
    if finish:
        message_refs = [refs.pop(0) for _ in range(nq)]
        acc, top = refs.pop(), refs.pop()
    else:
        acc, top = refs.pop(0), refs.pop(0)
    qt, ks, vt, key_at, seen = refs

    me = lax.axis_index("ctx")
    x, z, y = me // (Z * Y), (me // Y) % Z, me % Y
    row = x * Z + z
    row_low = row * ROW_SPAN
    row_high = row_low + (ROW_SPAN - 1)
    low = doc_start(lengths_ref, row_low)

    for n in range(nq):
        for h in range(HEADS):
            scaled = q_refs[n][:, h * DIM : (h + 1) * DIM].T.astype(jnp.float32) * EXP2_SCALE
            high = scaled.astype(jnp.bfloat16)
            qt[n * HEADS + h, :DIM] = high
            qt[n * HEADS + h, DIM:] = (scaled - high.astype(jnp.float32)).astype(jnp.bfloat16)

    for d in range(BAND + 2):
        seen[d] = 0
    for n in range(nb):
        key_at[n] = -FAR_ROW * ROW_SPAN
    starts, places_of = [], []
    for row_of in flat:
        row_from = row_of(x, z)
        k0 = row_from * ROW_SPAN + y * ROWS
        counts = (k0 <= row_high) & (k0 + (ROWS - 1) >= low)
        place = jnp.where(counts, row - row_from, BAND + 1)
        seen[place] = 1
        starts.append(k0)
        places_of.append(place)
    n_slots = jnp.int32(0)
    for d in range(BAND + 1):
        here = seen[d]
        seen[d] = n_slots
        n_slots = n_slots + here
    n = 0
    for ref, group in zip(kv_refs, places):
        for part in range(len(group)):

            @pl.when(places_of[n] <= BAND)
            def _(ref=ref, part=part, k0=starts[n], place=places_of[n]):
                slot = seen[place]
                base = 2 * part * ROWS
                key_at[slot] = k0
                at = pl.multiple_of(slot * ROWS, ROWS)
                for half in range(2):
                    ks[pl.ds(at, ROWS), half * DIM : (half + 1) * DIM] = ref[base : base + ROWS, :]
                for half in range(2):
                    rows = base + ROWS + half * DIM
                    vt[:DIM, pl.ds(pl.multiple_of(at + half * DIM, DIM), DIM)] = ref[rows : rows + DIM, :]

            n += 1
    vt[DIM:, :] = jnp.ones((EXT - DIM, nb * ROWS), jnp.bfloat16)

    if carried:
        acc[...] = acc_in[tile : tile + nq * HEADS]
        top[...] = top_in[tile : tile + nq * HEADS]
    else:
        acc[...] = jnp.zeros(acc.shape, jnp.float32)
        top[...] = jnp.full(top.shape, FLOOR, jnp.float32)

    def one_query_block(qb, _):
        t0 = qb * HEADS
        step = steps[0]
        for n in range(1, nq):
            step = jnp.where(qb == n, steps[n], step)
        q0 = row_low + ((y + step + Y) % Y) * ROWS
        first = doc_start(lengths_ref, q0)
        last = doc_start(lengths_ref, q0 + (ROWS - 1))

        def update(slot, count, masked):
            at = pl.ds(pl.multiple_of(slot * ROWS, ROWS), count * ROWS)
            k, v = ks[at, :], vt[:, at]
            if masked:
                query_pos = q0 + lax.broadcasted_iota(jnp.int32, (1, ROWS), 1)
                query_start = doc_start(lengths_ref, query_pos)
                key_pos = [
                    key_at[slot + i] + lax.broadcasted_iota(jnp.int32, (ROWS, ROWS), 0)
                    for i in range(count)
                ]
                key_pos = jnp.concatenate(key_pos, 0)
                allowed = (key_pos >= query_start) & (key_pos <= query_pos)
            olds = [top[t0 + h] for h in range(HEADS)]
            scores = [
                jnp.dot(k, qt[t0 + h], preferred_element_type=jnp.float32) for h in range(HEADS)
            ]
            if masked:
                scores = [jnp.where(allowed, s, NEG) for s in scores]
            news = [
                jnp.maximum(o, jnp.max(s, axis=0, keepdims=True)) for o, s in zip(olds, scores)
            ]
            weights = [
                jnp.exp2(s - n).astype(jnp.bfloat16) for s, n in zip(scores, news)
            ]
            sums = [jnp.dot(v, w, preferred_element_type=jnp.float32) for w in weights]
            sums = [
                acc[t0 + h] * jnp.exp2(olds[h] - news[h]) + sums[h]
                for h in range(HEADS)
            ]
            for h in range(HEADS):
                top[t0 + h] = news[h]
                acc[t0 + h] = sums[h]

        begin, near, inside, reach = (jnp.int32(0) for _ in range(4))
        for n in range(nb):
            k0 = key_at[n]
            begin = begin + jnp.where(k0 > q0 + (ROWS - 1), 1, 0)
            near = near + jnp.where(k0 + (ROWS - 1) > q0, 1, 0)
            inside = inside + jnp.where(k0 >= last, 1, 0)
            reach = reach + jnp.where(k0 + (ROWS - 1) >= first, 1, 0)

        def chunk(at, size):
            whole = (at >= near) & (at + size <= inside)
            pl.when(whole)(functools.partial(update, at, size, False))
            pl.when(jnp.logical_not(whole))(functools.partial(update, at, size, True))

        times = jnp.maximum(reach - begin, 0) // CHUNK

        def one_chunk(c, _):
            chunk(begin + c * CHUNK, CHUNK)
            return 0

        lax.fori_loop(0, times, one_chunk, 0)
        at = begin + times * CHUNK
        size = CHUNK // 2
        while size:
            some = reach - at >= size
            pl.when(some)(functools.partial(chunk, at, size))
            at = at + jnp.where(some, size, 0)
            size //= 2
        return 0

    lax.fori_loop(0, nq, one_query_block, 0)

    if finish:
        for n in range(nq):
            for h in range(HEADS):
                t = n * HEADS + h
                at = slice(h * ROWS, (h + 1) * ROWS)
                total = acc[t, DIM : DIM + 1]
                some = total > 0
                total = jnp.where(some, total, 1.0)
                log_norm = jnp.where(some, top[t] * LOG_2 + jnp.log(total), NEG)
                message_refs[n][:DIM, at] = (acc[t, :DIM] * (1.0 / total)).astype(jnp.bfloat16)
                first = log_norm.astype(jnp.bfloat16)
                rest = log_norm - first.astype(jnp.float32)
                second = rest.astype(jnp.bfloat16)
                third = (rest - second.astype(jnp.float32)).astype(jnp.bfloat16)
                row = lax.broadcasted_iota(jnp.int32, (EXT - DIM, ROWS), 0)
                pieces = jnp.where(
                    row == 0,
                    first.astype(jnp.float32),
                    jnp.where(row == 1, second.astype(jnp.float32), third.astype(jnp.float32)),
                )
                message_refs[n][DIM:, at] = pieces.astype(jnp.bfloat16)


def run_attend(lengths, queries, steps, arrays, places, carry, finish, tile=0):
    nq, nb = len(steps), sum(len(g) for g in places)
    tiles = nq * HEADS
    vmem = pl.BlockSpec(memory_space=pltpu.VMEM)
    acc = jax.ShapeDtypeStruct((tiles, EXT, ROWS), jnp.float32)
    top = jax.ShapeDtypeStruct((tiles, 1, ROWS), jnp.float32)
    scratch = [
        pltpu.VMEM((tiles, 2 * DIM, ROWS), jnp.bfloat16),
        pltpu.VMEM((nb * ROWS, 2 * DIM), jnp.bfloat16),
        pltpu.VMEM((EXT, nb * ROWS), jnp.bfloat16),
        pltpu.SMEM((nb,), jnp.int32),
        pltpu.SMEM((BAND + 2,), jnp.int32),
    ]
    if finish:
        out_shape = [jax.ShapeDtypeStruct((EXT, HEADS * ROWS), jnp.bfloat16)] * nq
        scratch += [pltpu.VMEM(top.shape, top.dtype), pltpu.VMEM(acc.shape, acc.dtype)]
    else:
        out_shape = [acc, top]
    operands = [lengths, *queries, *arrays, *(carry or ())]
    units = 5 * nq * nb * HEADS * ROWS * ROWS
    return pl.pallas_call(
        functools.partial(attend, steps, places, carry is not None, finish, tile),
        out_shape=out_shape,
        in_specs=[pl.BlockSpec(memory_space=pltpu.SMEM)] + [vmem] * (len(operands) - 1),
        out_specs=[vmem] * len(out_shape),
        scratch_shapes=scratch,
        compiler_params=pltpu.CompilerParams(vmem_limit_bytes=28 << 20),
        cost_estimate=pl.CostEstimate(
            flops=units * DIM * 2, bytes_accessed=1 << 20, transcendentals=units // 2
        ),
    )(*operands)


def turn_values(k_ref, v_ref, out_ref):
    out_ref[:ROWS, :] = k_ref[...]
    for half in range(2):
        at = ROWS + half * DIM
        out_ref[at : at + DIM, :] = v_ref[half * DIM : (half + 1) * DIM, :].T


def run_turn(kernel, shape, *operands):
    vmem = pl.BlockSpec(memory_space=pltpu.VMEM)
    return pl.pallas_call(
        kernel,
        out_shape=jax.ShapeDtypeStruct(shape, jnp.bfloat16),
        in_specs=[vmem] * len(operands),
        out_specs=vmem,
    )(*operands)


def merge(acc, top, *refs):
    *received, out, norm = refs
    for h in range(HEADS):
        at = slice(h * ROWS, (h + 1) * ROWS)
        own_total = acc[h, DIM : DIM + 1]
        logs = [top[h] * LOG_2 + jnp.log(own_total)]
        for r in received:
            pieces = r[DIM:, at].astype(jnp.float32)
            logs.append(pieces[0:1] + pieces[1:2] + pieces[2:3])
        most = functools.reduce(jnp.maximum, logs)
        parts = [jnp.exp(v - most) for v in logs]
        total = sum(parts)
        mixed = acc[h, :DIM] * (parts[0] / (own_total * total))
        for r, part in zip(received, parts[1:]):
            mixed = mixed + r[:DIM, at].astype(jnp.float32) * (part / total)
        out[:, h * DIM : (h + 1) * DIM] = mixed.T.astype(jnp.bfloat16)
        norm[h : h + 1, :] = most + jnp.log(total)


def run_merge(acc, top, received):
    vmem = pl.BlockSpec(memory_space=pltpu.VMEM)
    return pl.pallas_call(
        merge,
        out_shape=[
            jax.ShapeDtypeStruct((ROWS, HEADS * DIM), jnp.bfloat16),
            jax.ShapeDtypeStruct((HEADS, ROWS), jnp.float32),
        ],
        in_specs=[vmem] * (2 + len(received)),
        out_specs=[vmem] * 2,
        compiler_params=pltpu.CompilerParams(vmem_limit_bytes=24 << 20),
    )(acc, top, *received)


def shards(queries, keys, values, lengths):
    block = run_turn(turn_values, (2 * ROWS, DIM), keys, values)
    most, rest = gather(block)
    unzip = lambda pairs: ([a for a, _ in pairs], [p for _, p in pairs])
    steps = (-1, 1, 2)
    others = [lax.ppermute(queries, "ctx", y_pairs(-s)) for s in steps]
    received = []
    for low, high in ((0, 2), (2, 3)):
        group, these = steps[low:high], others[low:high]
        carry = run_attend(lengths, these, group, *unzip(most), None, False)
        messages = run_attend(lengths, these, group, *unzip(rest), carry, True)
        received += [lax.ppermute(m, "ctx", y_pairs(s)) for m, s in zip(messages, group)]
    acc, top = run_attend(lengths, [queries], (0,), *unzip(most + rest), None, False)
    return tuple(run_merge(acc, top, received))


def solution(mesh):
    in_specs = (P(("dp", "ctx"), None), P(("dp", "ctx"), None), P(("dp", "ctx"), None), P("dp"))
    out_specs = (P(("dp", "ctx"), None), P(None, ("dp", "ctx")))
    return jax.shard_map(shards, mesh=mesh, in_specs=in_specs, out_specs=out_specs, check_vma=False)
```

```python
import functools
import math

import jax
import jax.numpy as jnp
from jax import lax
from jax.experimental import pallas as pl
from jax.experimental.pallas import tpu as pltpu
from jax.sharding import PartitionSpec as P

X, Z, Y = 2, 8, 4
ROWS = 256
HEADS = 4
DIM = 128
EXT = DIM + 16
ROW_SPAN = Y * ROWS
BAND = 10
FAR_ROW = 1 << 14
NEG = -1e30
FLOOR = -1e29
CHUNK = 4
EXP2_SCALE = math.log2(math.e) / math.sqrt(DIM)
LOG_2 = math.log(2.0)


def index_of(x, z, y):
    return x * (Z * Y) + (z % Z) * Y + (y % Y)


def y_pairs(step):
    return [
        (index_of(x, z, y), index_of(x, z, y + step))
        for x in range(X)
        for z in range(Z)
        for y in range(Y)
    ]


COLUMNS = range(X)
NEXT = [((c, z), (c, z + 1)) for c in COLUMNS for z in range(Z - 1)]
LOW_NEXT = [((0, z), (1, (z + 1) % Z)) for z in range(Z)]
BACK = [((0, z), (1, z - 1)) for z in range(1, Z)] + [((c, 0), (c, Z - 1)) for c in COLUMNS]
HALF = [((c, z), (c, z + 4)) for c in COLUMNS for z in range(4)]
HALF += [((0, z), (1, z - 4)) for z in range(4, Z)]
EXTRA_ONE = [((c, 1), (c, Z - 1)) for c in COLUMNS]
EXTRA_FOUR = [((c, 4), (c, Z - 1)) for c in COLUMNS] + [((0, 3), (1, 0))]
UP = [((0, z), (0, z + 1)) for z in range(1, Z - 1)] + [((1, z), (1, (z + 1) % Z)) for z in range(Z)]
DOWN = [((0, z), (0, z - 1)) for z in range(4, Z)] + [((1, z), (1, (z - 1) % Z)) for z in range(Z)]


def move(block, pairs):
    along = [(index_of(*a, y), index_of(*b, y)) for a, b in pairs for y in range(Y)]
    return lax.ppermute(block, "ctx", along)


def own_row(step):
    return lambda x, z: x * Z + (z + step + Z) % Z


def low_row(step):
    return lambda x, z: jnp.where(x == 1, (z + step + Z) % Z, FAR_ROW)


def half_row(step):
    def row(x, z):
        at = x * Z + (z + step + Z) % Z - 4
        return jnp.where(at >= 0, at, FAR_ROW)

    return row


def back_row(step):
    def row(x, z):
        via = (z + step + Z) % Z
        return jnp.where(x == 1, via + 1, jnp.where(via == Z - 1, 0, FAR_ROW))

    return row


def extra_one_row(x, z):
    return jnp.where(z == Z - 1, x * Z + 1, FAR_ROW)


def extra_four_row(x, z):
    return jnp.where(z == Z - 1, x * Z + 4, jnp.where((z == 0) & (x == 1), 3, FAR_ROW))


def gather(block):
    below, low_next = move(block, NEXT), move(block, LOW_NEXT)
    back, half = move(block, BACK), move(block, HALF)
    extra_one, extra_four = move(block, EXTRA_ONE), move(block, EXTRA_FOUR)
    up = move(jnp.concatenate([below, low_next, half], 0), UP)
    down = move(jnp.concatenate([back, half, low_next], 0), DOWN)
    first = [
        (block, [own_row(0)]),
        (below, [own_row(-1)]),
        (low_next, [low_row(-1)]),
        (back, [back_row(0)]),
        (half, [half_row(0)]),
        (extra_one, [extra_one_row]),
        (extra_four, [extra_four_row]),
    ]
    second = [(up, [own_row(-2), low_row(-2), half_row(-1)]), (down, [back_row(1), half_row(1), low_row(0)])]
    return first, second


def doc_start(lengths_ref, position):
    start = position * 0
    end = jnp.int32(0)
    for k in range(8):
        size = lengths_ref[k]
        end = end + size
        start = start + jnp.where(position >= end, size, 0)
    return start


def attend(steps, places, carried, finish, tile, *refs):
    nq = len(steps)
    flat = [p for group in places for p in group]
    nb = len(flat)
    refs = list(refs)
    lengths_ref = refs.pop(0)
    q_refs = [refs.pop(0) for _ in range(1 if carried else nq)]
    kv_refs = [refs.pop(0) for _ in places]
    if carried:
        acc_in, top_in = refs.pop(0), refs.pop(0)
    if finish:
        message_refs = [refs.pop(0) for _ in range(nq)]
        acc, top = refs.pop(), refs.pop()
    else:
        acc, top = refs.pop(0), refs.pop(0)
    qt = q_refs[0] if carried else refs.pop(0)
    ks, vt, key_at, seen = refs

    me = lax.axis_index("ctx")
    x, z, y = me // (Z * Y), (me // Y) % Z, me % Y
    row = x * Z + z
    row_low = row * ROW_SPAN
    row_high = row_low + (ROW_SPAN - 1)
    low = doc_start(lengths_ref, row_low)

    for n in range(0 if carried else nq):
        for h in range(HEADS):
            scaled = q_refs[n][:, h * DIM : (h + 1) * DIM].T.astype(jnp.float32) * EXP2_SCALE
            high = scaled.astype(jnp.bfloat16)
            qt[n * HEADS + h, :DIM] = high
            qt[n * HEADS + h, DIM:] = (scaled - high.astype(jnp.float32)).astype(jnp.bfloat16)

    for d in range(BAND + 2):
        seen[d] = 0
    for n in range(nb):
        key_at[n] = -FAR_ROW * ROW_SPAN
    starts, places_of = [], []
    for row_of in flat:
        row_from = row_of(x, z)
        k0 = row_from * ROW_SPAN + y * ROWS
        counts = (k0 <= row_high) & (k0 + (ROWS - 1) >= low)
        place = jnp.where(counts, row - row_from, BAND + 1)
        seen[place] = 1
        starts.append(k0)
        places_of.append(place)
    n_slots = jnp.int32(0)
    for d in range(BAND + 1):
        here = seen[d]
        seen[d] = n_slots
        n_slots = n_slots + here
    n = 0
    for ref, group in zip(kv_refs, places):
        for part in range(len(group)):

            @pl.when(places_of[n] <= BAND)
            def _(ref=ref, part=part, k0=starts[n], place=places_of[n]):
                slot = seen[place]
                base = 2 * part * ROWS
                key_at[slot] = k0
                at = pl.multiple_of(slot * ROWS, ROWS)
                for half in range(2):
                    ks[pl.ds(at, ROWS), half * DIM : (half + 1) * DIM] = ref[base : base + ROWS, :]
                for half in range(2):
                    rows = base + ROWS + half * DIM
                    vt[:DIM, pl.ds(pl.multiple_of(at + half * DIM, DIM), DIM)] = ref[rows : rows + DIM, :]

            n += 1
    vt[DIM:, :] = jnp.ones((EXT - DIM, nb * ROWS), jnp.bfloat16)

    if carried:
        acc[...] = acc_in[tile : tile + nq * HEADS]
        top[...] = top_in[tile : tile + nq * HEADS]
    else:
        acc[...] = jnp.zeros(acc.shape, jnp.float32)
        top[...] = jnp.full(top.shape, FLOOR, jnp.float32)

    def one_query_block(qb, _):
        t0 = qb * HEADS
        step = steps[0]
        for n in range(1, nq):
            step = jnp.where(qb == n, steps[n], step)
        q0 = row_low + ((y + step + Y) % Y) * ROWS
        first = doc_start(lengths_ref, q0)
        last = doc_start(lengths_ref, q0 + (ROWS - 1))

        def update(slot, count, masked):
            at = pl.ds(pl.multiple_of(slot * ROWS, ROWS), count * ROWS)
            k, v = ks[at, :], vt[:, at]
            if masked:
                query_pos = q0 + lax.broadcasted_iota(jnp.int32, (1, ROWS), 1)
                query_start = doc_start(lengths_ref, query_pos)
                key_pos = [
                    key_at[slot + i] + lax.broadcasted_iota(jnp.int32, (ROWS, ROWS), 0)
                    for i in range(count)
                ]
                key_pos = jnp.concatenate(key_pos, 0)
                allowed = (key_pos >= query_start) & (key_pos <= query_pos)
            olds = [top[t0 + h] for h in range(HEADS)]
            scores = [
                jnp.dot(k, qt[t0 + h], preferred_element_type=jnp.float32) for h in range(HEADS)
            ]
            if masked:
                scores = [jnp.where(allowed, s, NEG) for s in scores]
            news = [
                jnp.maximum(o, jnp.max(s, axis=0, keepdims=True)) for o, s in zip(olds, scores)
            ]
            weights = [
                jnp.exp2(s - n).astype(jnp.bfloat16) for s, n in zip(scores, news)
            ]
            sums = [jnp.dot(v, w, preferred_element_type=jnp.float32) for w in weights]
            sums = [
                acc[t0 + h] * jnp.exp2(olds[h] - news[h]) + sums[h]
                for h in range(HEADS)
            ]
            for h in range(HEADS):
                top[t0 + h] = news[h]
                acc[t0 + h] = sums[h]

        begin, near, inside, reach = (jnp.int32(0) for _ in range(4))
        for n in range(nb):
            k0 = key_at[n]
            begin = begin + jnp.where(k0 > q0 + (ROWS - 1), 1, 0)
            near = near + jnp.where(k0 + (ROWS - 1) > q0, 1, 0)
            inside = inside + jnp.where(k0 >= last, 1, 0)
            reach = reach + jnp.where(k0 + (ROWS - 1) >= first, 1, 0)

        def chunk(at, size):
            whole = (at >= near) & (at + size <= inside)
            pl.when(whole)(functools.partial(update, at, size, False))
            pl.when(jnp.logical_not(whole))(functools.partial(update, at, size, True))

        times = jnp.maximum(reach - begin, 0) // CHUNK

        def one_chunk(c, _):
            chunk(begin + c * CHUNK, CHUNK)
            return 0

        lax.fori_loop(0, times, one_chunk, 0)
        at = begin + times * CHUNK
        size = CHUNK // 2
        while size:
            some = reach - at >= size
            pl.when(some)(functools.partial(chunk, at, size))
            at = at + jnp.where(some, size, 0)
            size //= 2
        return 0

    lax.fori_loop(0, nq, one_query_block, 0)

    if finish:
        for n in range(nq):
            for h in range(HEADS):
                t = n * HEADS + h
                at = slice(h * ROWS, (h + 1) * ROWS)
                total = acc[t, DIM : DIM + 1]
                some = total > 0
                total = jnp.where(some, total, 1.0)
                log_norm = jnp.where(some, top[t] * LOG_2 + jnp.log(total), NEG)
                message_refs[n][:DIM, at] = (acc[t, :DIM] * (1.0 / total)).astype(jnp.bfloat16)
                first = log_norm.astype(jnp.bfloat16)
                rest = log_norm - first.astype(jnp.float32)
                second = rest.astype(jnp.bfloat16)
                third = (rest - second.astype(jnp.float32)).astype(jnp.bfloat16)
                row = lax.broadcasted_iota(jnp.int32, (EXT - DIM, ROWS), 0)
                pieces = jnp.where(
                    row == 0,
                    first.astype(jnp.float32),
                    jnp.where(row == 1, second.astype(jnp.float32), third.astype(jnp.float32)),
                )
                message_refs[n][DIM:, at] = pieces.astype(jnp.bfloat16)


def run_attend(lengths, queries, steps, arrays, places, carry, finish, tile=0):
    nq, nb = len(steps), sum(len(g) for g in places)
    tiles = nq * HEADS
    vmem = pl.BlockSpec(memory_space=pltpu.VMEM)
    acc = jax.ShapeDtypeStruct((tiles, EXT, ROWS), jnp.float32)
    top = jax.ShapeDtypeStruct((tiles, 1, ROWS), jnp.float32)
    scratch = [
        pltpu.VMEM((nb * ROWS, 2 * DIM), jnp.bfloat16),
        pltpu.VMEM((EXT, nb * ROWS), jnp.bfloat16),
        pltpu.SMEM((nb,), jnp.int32),
        pltpu.SMEM((BAND + 2,), jnp.int32),
    ]
    if finish:
        out_shape = [jax.ShapeDtypeStruct((EXT, HEADS * ROWS), jnp.bfloat16)] * nq
        scratch += [pltpu.VMEM(top.shape, top.dtype), pltpu.VMEM(acc.shape, acc.dtype)]
    else:
        out_shape = [acc, top, jax.ShapeDtypeStruct((tiles, 2 * DIM, ROWS), jnp.bfloat16)]
    operands = [lengths, *queries, *arrays, *(carry or ())]
    units = 5 * nq * nb * HEADS * ROWS * ROWS
    return pl.pallas_call(
        functools.partial(attend, steps, places, carry is not None, finish, tile),
        out_shape=out_shape,
        in_specs=[pl.BlockSpec(memory_space=pltpu.SMEM)] + [vmem] * (len(operands) - 1),
        out_specs=[vmem] * len(out_shape),
        scratch_shapes=scratch,
        compiler_params=pltpu.CompilerParams(vmem_limit_bytes=20 << 20),
        cost_estimate=pl.CostEstimate(
            flops=units * DIM * 2, bytes_accessed=1 << 20, transcendentals=units // 2
        ),
    )(*operands)


def turn_values(k_ref, v_ref, out_ref):
    out_ref[:ROWS, :] = k_ref[...]
    for half in range(2):
        at = ROWS + half * DIM
        out_ref[at : at + DIM, :] = v_ref[half * DIM : (half + 1) * DIM, :].T


def run_turn(kernel, shape, *operands):
    vmem = pl.BlockSpec(memory_space=pltpu.VMEM)
    return pl.pallas_call(
        kernel,
        out_shape=jax.ShapeDtypeStruct(shape, jnp.bfloat16),
        in_specs=[vmem] * len(operands),
        out_specs=vmem,
    )(*operands)


def merge(acc, top, *refs):
    *received, out, norm = refs
    for h in range(HEADS):
        at = slice(h * ROWS, (h + 1) * ROWS)
        own_total = acc[h, DIM : DIM + 1]
        logs = [top[h] * LOG_2 + jnp.log(own_total)]
        for r in received:
            pieces = r[DIM:, at].astype(jnp.float32)
            logs.append(pieces[0:1] + pieces[1:2] + pieces[2:3])
        most = functools.reduce(jnp.maximum, logs)
        parts = [jnp.exp(v - most) for v in logs]
        total = sum(parts)
        mixed = acc[h, :DIM] * (parts[0] / (own_total * total))
        for r, part in zip(received, parts[1:]):
            mixed = mixed + r[:DIM, at].astype(jnp.float32) * (part / total)
        out[:, h * DIM : (h + 1) * DIM] = mixed.T.astype(jnp.bfloat16)
        norm[h : h + 1, :] = most + jnp.log(total)


def run_merge(acc, top, received):
    vmem = pl.BlockSpec(memory_space=pltpu.VMEM)
    return pl.pallas_call(
        merge,
        out_shape=[
            jax.ShapeDtypeStruct((ROWS, HEADS * DIM), jnp.bfloat16),
            jax.ShapeDtypeStruct((HEADS, ROWS), jnp.float32),
        ],
        in_specs=[vmem] * (2 + len(received)),
        out_specs=[vmem] * 2,
        compiler_params=pltpu.CompilerParams(vmem_limit_bytes=24 << 20),
    )(acc, top, *received)


def shards(queries, keys, values, lengths):
    block = run_turn(turn_values, (2 * ROWS, DIM), keys, values)
    most, rest = gather(block)
    unzip = lambda pairs: ([a for a, _ in pairs], [p for _, p in pairs])
    steps = (-1, 1, 2)
    others = [lax.ppermute(queries, "ctx", y_pairs(-s)) for s in steps]
    received = []
    for low, high in ((0, 2), (2, 3)):
        group, these = steps[low:high], others[low:high]
        *carry, turned = run_attend(lengths, these, group, *unzip(most), None, False)
        messages = run_attend(lengths, [turned], group, *unzip(rest), carry, True)
        received += [lax.ppermute(m, "ctx", y_pairs(s)) for m, s in zip(messages, group)]
    acc, top, _ = run_attend(lengths, [queries], (0,), *unzip(most + rest), None, False)
    return tuple(run_merge(acc, top, received))


def solution(mesh):
    in_specs = (P(("dp", "ctx"), None), P(("dp", "ctx"), None), P(("dp", "ctx"), None), P("dp"))
    out_specs = (P(("dp", "ctx"), None), P(None, ("dp", "ctx")))
    return jax.shard_map(shards, mesh=mesh, in_specs=in_specs, out_specs=out_specs, check_vma=False)
```
